32 devices in a mesh: dp: 16 (over z, y, core), mp: 2 (over x).
Axes of the slice: x: 2, y: 2, z: 4, core: 2. Of those that a mesh axis runs over, the one named last changes fastest.
Arguments:
- queries: bfloat16 [12288, 6144], P('dp', 'mp'), may hold values from -20 to 20
- keys: bfloat16 [12288, 6144], P('dp', 'mp'), may hold values from -20 to 20
- values: bfloat16 [12288, 6144], P('dp', 'mp'), may hold values from -12 to 12
- patch_counts: int32 [64], replicated, may hold values from 1 to 768, 12288 in all
- out_weight: bfloat16 [6144, 6144], P('mp', 'dp'), may hold values from -0.078125 to 0.078125
Outputs:
- projected: bfloat16 [12288, 6144], P(('dp', 'mp'))
The draws below stay inside these ranges and needn't reach their ends.
Inputs may be any that keep to these rules, and one draw needn't show every extreme that they name: `patch_counts`: the counts sum to 12288; the largest is exactly 768.
All inputs are finite; a program needn't handle non-finite values.
Results may differ from the reference program's by a relative error of at most 0.0066.
Values may be sent and summed in bfloat16 or wider, within the bound.
A program may use at most 256 MiB of HBM per device.

```python
import math
import jax
import jax.numpy as jnp
import numpy as np
from jax import lax

D = 6144
HEADS = 48
HEAD_DIM = 128
TOK_DEV = 768
TOKENS = 12288
IMAGES = 64
N_DP = 16
N_MP = 2


def draw_queries(key, part):
    key = jax.random.fold_in(key, 5)
    fresh = jnp.clip(jax.random.normal(key, (TOKENS, HEADS * HEAD_DIM), jnp.float32), -4.0, 4.0)
    return fresh.astype(jnp.bfloat16)


def draw_keys(key, part):
    key = jax.random.fold_in(key, 9)
    fresh = jnp.clip(jax.random.normal(key, (TOKENS, HEADS * HEAD_DIM), jnp.float32), -4.0, 4.0)
    return fresh.astype(jnp.bfloat16)


def block_scale(key, shape, shards, least, top_value):
    level = 1.0
    for axis_at, blocks in shards:
        steps = jax.random.uniform(jax.random.fold_in(jax.random.fold_in(key, 6), axis_at), (blocks,), jnp.float32, least / len(shards), top_value / len(shards))
        level = level * jnp.repeat(jnp.exp(steps), shape[axis_at] // blocks).reshape((-1,) + (1,) * (len(shape) - 1 - axis_at))
    return level


def length_profile(amount, total, most, slope):
    portions = [(1 << 20) // math.isqrt(grade ** slope) + 1 for grade in range(2, amount + 1)]
    spare, counts = total - most - (amount - 1), [1] * (amount - 1)
    while spare > 0:
        free = [i for i in range(amount - 1) if counts[i] < most]
        pool, left = sum([portions[i] for i in free]), spare
        for i in free:
            addition = min(most - counts[i], max(1, left * portions[i] // pool), spare)
            counts[i] = counts[i] + addition
            spare = spare - addition
    return np.array([most] + counts)


def ragged(rng, amount, total, most, lean):
    if amount == 2:
        one = jax.random.randint(rng, (), max(1, total - most), min(most, total - 1) + 1)
        return jnp.stack([one, total - one])
    lengths = jnp.asarray(length_profile(amount, total, most, lean), jnp.int32)
    couples = (amount - 1) // 2
    donor, sink = lengths[1:1 + 2 * couples:2], lengths[2:2 + 2 * couples:2]
    slack = jnp.minimum(donor - 1, most - sink)
    moved = jax.random.randint(jax.random.fold_in(rng, 1), (couples,), 0, 1 << 20) % (slack + 1)
    lengths = lengths.at[1:1 + 2 * couples:2].set(donor - moved).at[2:2 + 2 * couples:2].set(sink + moved)
    return lengths[jax.random.permutation(jax.random.fold_in(rng, 2), amount)]


def bell_draw(rng, dims, width, most, pieces=(), held_as=jnp.bfloat16):
    drawn = jax.random.normal(rng, dims, jnp.float32) * width
    if len(pieces) > 0:
        drawn = block_scale(rng, dims, pieces, -0.22, 0.18) * drawn
    return jnp.clip(drawn, min=-most, max=most).astype(held_as)


def setup_inputs(seed: int = 0) -> dict:
    splits = jax.random.split(jax.random.key(seed), 6)
    return {
        "queries": draw_queries(jax.random.fold_in(splits[5], 71), 0),
        "keys": draw_keys(jax.random.fold_in(splits[5], 71), 0),
        "values": bell_draw(splits[2], (TOKENS, HEADS * HEAD_DIM), 2.0, 12.0, ((0, 16), (1, 2))),
        "patch_counts": ragged(splits[3], IMAGES, TOKENS, TOK_DEV, 2).astype(jnp.int32),
        "out_weight": bell_draw(splits[4], (HEADS * HEAD_DIM, D), (HEADS * HEAD_DIM) ** -0.5, 0.078125, ((0, 2), (1, 16))),
    }


def image_index(positions, starts):
    return jnp.sum((starts[None, :] <= positions[:, None]).astype(jnp.int32), axis=1) - 1


def attend_block(q_block, k_window, v_window, same_image):
    head_count = q_block.shape[1] // HEAD_DIM

    def one_head(head_index):
        q_head = lax.dynamic_slice_in_dim(q_block, head_index * HEAD_DIM, HEAD_DIM, 1)
        k_head = lax.dynamic_slice_in_dim(k_window, head_index * HEAD_DIM, HEAD_DIM, 1)
        v_head = lax.dynamic_slice_in_dim(v_window, head_index * HEAD_DIM, HEAD_DIM, 1)
        scores = jnp.dot(q_head, k_head.T, preferred_element_type=jnp.float32) * (HEAD_DIM ** -0.5)
        scores = jnp.where(same_image, scores, jnp.float32(-1e30))
        row_max = jnp.max(scores, axis=1, keepdims=True)
        lifted = jnp.exp(scores - row_max)
        row_total = jnp.sum(lifted, axis=1, keepdims=True)
        weights = (lifted / row_total).astype(jnp.bfloat16)
        return jnp.dot(weights, v_head, preferred_element_type=jnp.float32).astype(jnp.bfloat16)

    per_head = lax.map(one_head, jnp.arange(head_count).astype(jnp.int32))
    return jnp.transpose(per_head, (1, 0, 2)).reshape(q_block.shape[0], head_count * HEAD_DIM)


def reference(queries, keys, values, patch_counts, out_weight):
    starts = jnp.cumsum(patch_counts).astype(jnp.int32) - patch_counts
    padding = jnp.zeros((TOK_DEV, queries.shape[1]), jnp.bfloat16)
    keys_padded = jnp.concatenate([padding, keys, padding], axis=0)
    values_padded = jnp.concatenate([padding, values, padding], axis=0)

    def query_block(block_index):
        row_first = block_index * TOK_DEV
        q_block = lax.dynamic_slice_in_dim(queries, row_first, TOK_DEV, 0)
        k_window = lax.dynamic_slice_in_dim(keys_padded, row_first, 3 * TOK_DEV, 0)
        v_window = lax.dynamic_slice_in_dim(values_padded, row_first, 3 * TOK_DEV, 0)
        q_pos = (row_first + jnp.arange(TOK_DEV)).astype(jnp.int32)
        k_pos = (row_first - TOK_DEV + jnp.arange(3 * TOK_DEV)).astype(jnp.int32)
        k_valid = (k_pos >= 0) & (k_pos < TOKENS)
        same_image = (image_index(q_pos, starts)[:, None] == image_index(k_pos, starts)[None, :]) & k_valid[None, :]
        return attend_block(q_block, k_window, v_window, same_image)

    attended = lax.map(query_block, jnp.arange(N_DP).astype(jnp.int32)).reshape(TOKENS, queries.shape[1])
    group_width = queries.shape[1] // N_MP

    def add_group(carry, group_index):
        cols = lax.dynamic_slice_in_dim(attended, group_index * group_width, group_width, 1)
        rows_w = lax.dynamic_slice_in_dim(out_weight, group_index * group_width, group_width, 0)
        partial_value = jnp.dot(cols, rows_w, preferred_element_type=jnp.float32).astype(jnp.bfloat16)
        partial_value = lax.optimization_barrier(partial_value)
        return carry + partial_value.astype(jnp.float32), None

    summed, _ = lax.scan(add_group, jnp.zeros((TOKENS, D), jnp.float32), jnp.arange(N_MP).astype(jnp.int32))
    return summed.astype(jnp.bfloat16)
```

```python
import functools

import jax
import jax.numpy as jnp
from jax import lax
from jax.experimental import pallas as pl
from jax.experimental.pallas import tpu as pltpu
from jax.sharding import PartitionSpec as P

HEAD_DIM = 128
Q_ROWS = 256
K_ROWS = 256
CHUNKS = 3
LOG2E = 1.4426950408889634


def attend_kernel(span_ref, q_ref, kb_ref, k_ref, ka_ref, vb_ref, v_ref, va_ref, qseg_ref, kseg_ref, out_ref,
                  acc_ref, max_ref, *, heads, rows):
    factor = HEAD_DIM ** (-0.5) * LOG2E
    per_part = rows // K_ROWS
    ones = jnp.ones((K_ROWS, HEAD_DIM), jnp.bfloat16)

    def q_step(qi, _):
        q_at = pl.ds(pl.multiple_of(qi * Q_ROWS, Q_ROWS), Q_ROWS)
        acc_ref[...] = jnp.zeros_like(acc_ref)
        max_ref[...] = jnp.full_like(max_ref, -1e30)
        qseg = qseg_ref[q_at, :]
        qseg = jnp.concatenate([qseg] * (K_ROWS // 128), axis=1)
        low, high = span_ref[0, qi], span_ref[1, qi]

        for part, (kk, vv) in enumerate(((kb_ref, vb_ref), (k_ref, v_ref), (ka_ref, va_ref))):
            def k_step(ki, _, part=part, kk=kk, vv=vv):
                k_at = pl.ds(pl.multiple_of(ki * K_ROWS, K_ROWS), K_ROWS)
                same = qseg == kseg_ref[part * per_part + ki]
                for h in range(heads):
                    cols = pl.ds(h * HEAD_DIM, HEAD_DIM)
                    s = lax.dot_general(q_ref[q_at, cols], kk[k_at, cols], (((1,), (1,)), ((), ())),
                                        preferred_element_type=jnp.float32) * factor
                    s = jnp.where(same, s, -1e30)
                    old = max_ref[h]
                    new = jnp.maximum(old, jnp.max(s, axis=1, keepdims=True))
                    max_ref[h] = new
                    wide = jnp.concatenate([new] * (K_ROWS // 128), axis=1)
                    p = jnp.exp2(s - wide).astype(jnp.bfloat16)
                    fade = jnp.exp2(old - new)
                    v_ext = jnp.concatenate([vv[k_at, cols], ones], axis=1)
                    acc_ref[h] = acc_ref[h] * jnp.concatenate([fade, fade], axis=1) + jnp.dot(
                        p, v_ext, preferred_element_type=jnp.float32)
                return 0

            first = jnp.clip(low - part * per_part, 0, per_part)
            last = jnp.clip(high - part * per_part, 0, per_part)
            lax.fori_loop(first, last, k_step, 0)
        for h in range(heads):
            acc = acc_ref[h]
            out_ref[q_at, h * HEAD_DIM:(h + 1) * HEAD_DIM] = (
                acc[:, :HEAD_DIM] / acc[:, HEAD_DIM:]).astype(jnp.bfloat16)
        return 0

    lax.fori_loop(0, rows // Q_ROWS, q_step, 0)


def attend(span, queries, keys, values, before, after, q_seg, k_seg, chunk, width):
    rows = queries.shape[0]
    heads = next(n for n in (4, 3, 2, 1) if (width // HEAD_DIM) % n == 0)
    block = heads * HEAD_DIM
    steps = width // block
    whole = pl.BlockSpec((rows, block), lambda i, s: (0, chunk * steps + i))
    k_part = pl.BlockSpec((rows, block), lambda i, s: (0, i))
    v_part = pl.BlockSpec((rows, block), lambda i, s: (0, steps + i))
    return pl.pallas_call(
        functools.partial(attend_kernel, heads=heads, rows=rows),
        grid_spec=pltpu.PrefetchScalarGridSpec(
            num_scalar_prefetch=1,
            grid=(steps,),
            in_specs=[whole, k_part, whole, k_part, v_part, whole, v_part,
                      pl.BlockSpec((rows, 128), lambda i, s: (0, 0)),
                      pl.BlockSpec((3 * rows // K_ROWS, 1, K_ROWS), lambda i, s: (0, 0, 0))],
            out_specs=pl.BlockSpec((rows, block), lambda i, s: (0, i)),
            scratch_shapes=[pltpu.VMEM((heads, Q_ROWS, 2 * HEAD_DIM), jnp.float32),
                            pltpu.VMEM((heads, Q_ROWS, HEAD_DIM), jnp.float32)],
        ),
        out_shape=jax.ShapeDtypeStruct((rows, width), jnp.bfloat16),
        compiler_params=pltpu.CompilerParams(vmem_limit_bytes=40 * 2 ** 20),
        cost_estimate=pl.CostEstimate(flops=4 * rows * rows * width, bytes_accessed=16 * rows * width,
                                      transcendentals=rows * rows * width // HEAD_DIM),
    )(span, queries, before, keys, after, before, values, after, q_seg, k_seg)


def shards(queries, keys, values, patch_counts, out_weight):
    rows, columns = queries.shape
    devices, groups = lax.axis_size("dp"), lax.axis_size("mp")
    width = columns // CHUNKS
    up = [(i, i + 1) for i in range(devices - 1)]
    down = [(j, i) for i, j in up]

    halos = []
    for c in range(CHUNKS):
        at = slice(c * width, (c + 1) * width)
        pair = jnp.concatenate([keys[:, at], values[:, at]], axis=1)
        if halos:
            pair, _ = lax.optimization_barrier((pair, halos[-1][0][:8, :128]))
        halos.append((lax.ppermute(pair, "dp", up), lax.ppermute(pair, "dp", down)))

    row_first = lax.axis_index("dp") * rows
    total_rows = devices * rows
    ends = jnp.cumsum(patch_counts)
    starts = ends - patch_counts
    k_pos = row_first - rows + jnp.arange(3 * rows, dtype=jnp.int32)
    seg = jnp.sum((starts[None, :] <= k_pos[:, None]).astype(jnp.int32), axis=1) - 1
    seg = jnp.where((k_pos >= 0) & (k_pos < total_rows), seg, -1)
    q_seg = jnp.broadcast_to(seg[rows:2 * rows, None], (rows, 128))
    k_seg = seg.reshape(3 * rows // K_ROWS, 1, K_ROWS)
    q_first = row_first + jnp.arange(rows // Q_ROWS, dtype=jnp.int32) * Q_ROWS
    low = jnp.max(jnp.where(starts[None, :] <= q_first[:, None], starts[None, :], 0), axis=1)
    q_last = q_first + Q_ROWS - 1
    high = jnp.min(jnp.where(ends[None, :] > q_last[:, None], ends[None, :], total_rows), axis=1)
    low = jnp.clip((low - row_first + rows) // K_ROWS, 0, 3 * rows // K_ROWS)
    high = jnp.clip((high - row_first + rows + K_ROWS - 1) // K_ROWS, 0, 3 * rows // K_ROWS)
    span = jnp.stack([low, high]).astype(jnp.int32)

    attended = jnp.concatenate(
        [attend(span, queries, keys, values, *halos[c], q_seg, k_seg, c, width) for c in range(CHUNKS)], axis=1)

    part = out_weight.shape[1] // CHUNKS
    block = rows // groups
    me = lax.axis_index("mp")
    done = []
    for c in range(CHUNKS):
        piece = out_weight[:, c * part:(c + 1) * part]
        if c == 1:
            piece, _ = lax.optimization_barrier((piece, halos[-1][0][:8, :128]))
        gathered = lax.all_gather(piece, "dp", axis=1, tiled=True)
        partial_value = jnp.dot(attended, gathered, preferred_element_type=jnp.float32).astype(jnp.bfloat16)
        total = lax.dynamic_slice_in_dim(partial_value, me * block, block, 0).astype(jnp.float32)
        for k in range(1, groups):
            theirs = lax.dynamic_slice_in_dim(partial_value, ((me + k) % groups) * block, block, 0)
            got = lax.ppermute(theirs, "mp", [(i, (i + k) % groups) for i in range(groups)])
            total = total + got.astype(jnp.float32)
        done.append(total.astype(jnp.bfloat16).reshape(block, devices, 1, part))
    return jnp.concatenate(done, axis=2).reshape(block, devices * CHUNKS * part)


def solution(mesh):
    placed = (P("dp", "mp"), P("dp", "mp"), P("dp", "mp"), P(), P("mp", "dp"))
    return jax.shard_map(
        shards, mesh=mesh, in_specs=placed, out_specs=P(("dp", "mp"), None), check_vma=False
    )
```

```python
import functools

import jax
import jax.numpy as jnp
from jax import lax
from jax.experimental import pallas as pl
from jax.experimental.pallas import tpu as pltpu
from jax.sharding import PartitionSpec as P

HEAD_DIM = 128
Q_ROWS = 256
K_ROWS = 256
CHUNKS = 3
LOG2E = 1.4426950408889634


def attend_kernel(span_ref, q_ref, kb_ref, k_ref, ka_ref, vb_ref, v_ref, va_ref, qseg_ref, kseg_ref, out_ref,
                  acc_ref, max_ref, *, heads, rows):
    factor = HEAD_DIM ** (-0.5) * LOG2E
    per_part = rows // K_ROWS
    ones = jnp.ones((K_ROWS, HEAD_DIM), jnp.bfloat16)

    def q_step(qi, _):
        q_at = pl.ds(pl.multiple_of(qi * Q_ROWS, Q_ROWS), Q_ROWS)
        acc_ref[...] = jnp.zeros_like(acc_ref)
        max_ref[...] = jnp.full_like(max_ref, -1e30)
        qseg = qseg_ref[q_at, :]
        qseg = jnp.concatenate([qseg] * (K_ROWS // 128), axis=1)
        low, high = span_ref[0, qi], span_ref[1, qi]

        for part, (kk, vv) in enumerate(((kb_ref, vb_ref), (k_ref, v_ref), (ka_ref, va_ref))):
            def k_step(ki, _, part=part, kk=kk, vv=vv):
                k_at = pl.ds(pl.multiple_of(ki * K_ROWS, K_ROWS), K_ROWS)
                same = qseg == kseg_ref[part * per_part + ki]
                for h in range(heads):
                    cols = pl.ds(h * HEAD_DIM, HEAD_DIM)
                    s = lax.dot_general(q_ref[q_at, cols], kk[k_at, cols], (((1,), (1,)), ((), ())),
                                        preferred_element_type=jnp.float32) * factor
                    s = jnp.where(same, s, -1e30)
                    old = max_ref[h]
                    new = jnp.maximum(old, jnp.max(s, axis=1, keepdims=True))
                    max_ref[h] = new
                    wide = jnp.concatenate([new] * (K_ROWS // 128), axis=1)
                    p = jnp.exp2(s - wide).astype(jnp.bfloat16)
                    fade = jnp.exp2(old - new)
                    v_ext = jnp.concatenate([vv[k_at, cols], ones], axis=1)
                    acc_ref[h] = acc_ref[h] * jnp.concatenate([fade, fade], axis=1) + jnp.dot(
                        p, v_ext, preferred_element_type=jnp.float32)
                return 0

            first = jnp.clip(low - part * per_part, 0, per_part)
            last = jnp.clip(high - part * per_part, 0, per_part)
            lax.fori_loop(first, last, k_step, 0)
        for h in range(heads):
            acc = acc_ref[h]
            out_ref[q_at, h * HEAD_DIM:(h + 1) * HEAD_DIM] = (
                acc[:, :HEAD_DIM] / acc[:, HEAD_DIM:]).astype(jnp.bfloat16)
        return 0

    lax.fori_loop(0, rows // Q_ROWS, q_step, 0)


def attend(span, queries, keys, values, before, after, q_seg, k_seg, chunk, width):
    rows = queries.shape[0]
    heads = next(n for n in (4, 3, 2, 1) if (width // HEAD_DIM) % n == 0)
    block = heads * HEAD_DIM
    steps = width // block
    whole = pl.BlockSpec((rows, block), lambda i, s: (0, chunk * steps + i))
    k_part = pl.BlockSpec((rows, block), lambda i, s: (0, i))
    v_part = pl.BlockSpec((rows, block), lambda i, s: (0, steps + i))
    return pl.pallas_call(
        functools.partial(attend_kernel, heads=heads, rows=rows),
        grid_spec=pltpu.PrefetchScalarGridSpec(
            num_scalar_prefetch=1,
            grid=(steps,),
            in_specs=[whole, k_part, whole, k_part, v_part, whole, v_part,
                      pl.BlockSpec((rows, 128), lambda i, s: (0, 0)),
                      pl.BlockSpec((3 * rows // K_ROWS, 1, K_ROWS), lambda i, s: (0, 0, 0))],
            out_specs=pl.BlockSpec((rows, block), lambda i, s: (0, i)),
            scratch_shapes=[pltpu.VMEM((heads, Q_ROWS, 2 * HEAD_DIM), jnp.float32),
                            pltpu.VMEM((heads, Q_ROWS, HEAD_DIM), jnp.float32)],
        ),
        out_shape=jax.ShapeDtypeStruct((rows, width), jnp.bfloat16),
        compiler_params=pltpu.CompilerParams(vmem_limit_bytes=40 * 2 ** 20),
        cost_estimate=pl.CostEstimate(flops=4 * rows * rows * width, bytes_accessed=16 * rows * width,
                                      transcendentals=rows * rows * width // HEAD_DIM),
    )(span, queries, before, keys, after, before, values, after, q_seg, k_seg)


def shards(queries, keys, values, patch_counts, out_weight):
    rows, columns = queries.shape
    devices, groups = lax.axis_size("dp"), lax.axis_size("mp")
    width = columns // CHUNKS
    up = [(i, i + 1) for i in range(devices - 1)]
    down = [(j, i) for i, j in up]

    halos = []
    for c in range(CHUNKS):
        at = slice(c * width, (c + 1) * width)
        pair = jnp.concatenate([keys[:, at], values[:, at]], axis=1)
        if halos:
            pair, _ = lax.optimization_barrier((pair, halos[-1][0][:8, :128]))
        halos.append((lax.ppermute(pair, "dp", up), lax.ppermute(pair, "dp", down)))

    row_first = lax.axis_index("dp") * rows
    total_rows = devices * rows
    ends = jnp.cumsum(patch_counts)
    starts = ends - patch_counts
    k_pos = row_first - rows + jnp.arange(3 * rows, dtype=jnp.int32)
    seg = jnp.sum((starts[None, :] <= k_pos[:, None]).astype(jnp.int32), axis=1) - 1
    seg = jnp.where((k_pos >= 0) & (k_pos < total_rows), seg, -1)
    q_seg = jnp.broadcast_to(seg[rows:2 * rows, None], (rows, 128))
    k_seg = seg.reshape(3 * rows // K_ROWS, 1, K_ROWS)
    q_first = row_first + jnp.arange(rows // Q_ROWS, dtype=jnp.int32) * Q_ROWS
    low = jnp.max(jnp.where(starts[None, :] <= q_first[:, None], starts[None, :], 0), axis=1)
    q_last = q_first + Q_ROWS - 1
    high = jnp.min(jnp.where(ends[None, :] > q_last[:, None], ends[None, :], total_rows), axis=1)
    low = jnp.clip((low - row_first + rows) // K_ROWS, 0, 3 * rows // K_ROWS)
    high = jnp.clip((high - row_first + rows + K_ROWS - 1) // K_ROWS, 0, 3 * rows // K_ROWS)
    span = jnp.stack([low, high]).astype(jnp.int32)

    chips = devices // 2
    ring = list(range(0, chips, 2)) + list(range(chips - 1 - chips % 2, 0, -2))
    onward = [(ring[i], ring[(i + 1) % chips]) for i in range(chips)]
    turn = [(2 * a, 2 * b) for a, b in onward] + [(2 * b + 1, 2 * a + 1) for a, b in onward]
    swap = [(i, i ^ 1) for i in range(devices)]
    part = out_weight.shape[1]
    block = rows // groups
    me = lax.axis_index("mp")

    own, other = [], []
    for c in range(CHUNKS):
        own.append(attend(span, queries, keys, values, *halos[c], q_seg, k_seg, c, width))
        other.append(lax.ppermute(own[-1], "dp", swap))
    both = jnp.concatenate([jnp.concatenate(own, axis=1), jnp.concatenate(other, axis=1)], axis=0)

    weight = out_weight
    mine, theirs, batch = [], [], []
    for step in range(chips):
        if step:
            weight = lax.ppermute(weight, "dp", turn)
        partial_value = jnp.dot(both, weight, preferred_element_type=jnp.float32)
        partial_value = partial_value.astype(jnp.bfloat16).reshape(2, groups, block, part)
        total = lax.dynamic_index_in_dim(partial_value, me, 1, False).astype(jnp.float32)
        for k in range(1, groups):
            away = lax.dynamic_index_in_dim(partial_value, (me + k) % groups, 1, False)
            got = lax.ppermute(away, "mp", [(i, (i + k) % groups) for i in range(groups)])
            total = total + got.astype(jnp.float32)
        total = total.astype(jnp.bfloat16)
        mine.append(total[0])
        batch.append(total[1])
        if step % (chips // 2) == chips // 2 - 1:
            theirs.append(lax.ppermute(jnp.stack(batch), "dp", swap))
            batch = []
    mine, theirs = jnp.stack(mine), jnp.concatenate(theirs, axis=0)

    place = jnp.array([ring.index(c) for c in range(chips)], jnp.int32)
    index = lax.axis_index("dp")
    core, at = index % 2, place[index // 2]
    owner = jnp.arange(devices, dtype=jnp.int32)
    ahead = (at - place[owner // 2]) % chips
    behind = (place[owner // 2] - at) % chips
    step_of = jnp.where(owner % 2 == 0, ahead, behind)
    return assemble(mine, theirs, step_of, core)


def assemble_kernel(mine_at, theirs_at, core_ref, mine_ref, theirs_ref, out_ref):
    is_mine = pl.program_id(0) % 2 == core_ref[0]

    @pl.when(is_mine)
    def _():
        out_ref[...] = mine_ref[0]

    @pl.when(jnp.logical_not(is_mine))
    def _():
        out_ref[...] = theirs_ref[0]


def assemble(mine, theirs, step_of, core):
    chips, block, part = mine.shape
    devices = 2 * chips
    if part % 128:
        owner = jnp.arange(devices, dtype=jnp.int32)
        pieces = jnp.concatenate([mine, theirs], axis=0)
        pieces = pieces[step_of + jnp.where(owner % 2 == core, 0, chips)]
        return jnp.transpose(pieces, (1, 0, 2)).reshape(block, devices * part)
    pairs = step_of.reshape(chips, 2)
    mine_at = jnp.repeat(jnp.where(core == 0, pairs[:, 0], pairs[:, 1]), 2)
    theirs_at = jnp.repeat(jnp.where(core == 0, pairs[:, 1], pairs[:, 0]), 2)
    return pl.pallas_call(
        assemble_kernel,
        grid_spec=pltpu.PrefetchScalarGridSpec(
            num_scalar_prefetch=3,
            grid=(devices,),
            in_specs=[pl.BlockSpec((1, block, part), lambda d, m, t, c: (m[d], 0, 0)),
                      pl.BlockSpec((1, block, part), lambda d, m, t, c: (t[d], 0, 0))],
            out_specs=pl.BlockSpec((block, part), lambda d, m, t, c: (0, d)),
        ),
        out_shape=jax.ShapeDtypeStruct((block, devices * part), jnp.bfloat16),
        cost_estimate=pl.CostEstimate(flops=0, bytes_accessed=4 * block * devices * part, transcendentals=0),
    )(mine_at, theirs_at, core[None].astype(jnp.int32), mine, theirs)


def solution(mesh):
    placed = (P("dp", "mp"), P("dp", "mp"), P("dp", "mp"), P(), P("mp", "dp"))
    return jax.shard_map(
        shards, mesh=mesh, in_specs=placed, out_specs=P(("dp", "mp"), None), check_vma=False
    )
```

```python
import functools

import jax
import jax.numpy as jnp
from jax import lax
from jax.experimental import pallas as pl
from jax.experimental.pallas import tpu as pltpu
from jax.sharding import PartitionSpec as P

HEAD_DIM = 128
Q_ROWS = 256
K_ROWS = 256
CHUNKS = 2
LOG2E = 1.4426950408889634


def attend_kernel(span_ref, q_ref, kb_ref, k_ref, ka_ref, vb_ref, v_ref, va_ref, qseg_ref, kseg_ref, out_ref,
                  acc_ref, max_ref, *, heads, rows):
    factor = HEAD_DIM ** (-0.5) * LOG2E
    per_part = rows // K_ROWS
    ones = jnp.ones((K_ROWS, HEAD_DIM), jnp.bfloat16)

    def q_step(qi, _):
        q_at = pl.ds(pl.multiple_of(qi * Q_ROWS, Q_ROWS), Q_ROWS)
        acc_ref[...] = jnp.zeros_like(acc_ref)
        max_ref[...] = jnp.full_like(max_ref, -1e30)
        qseg = qseg_ref[q_at, :]
        qseg = jnp.concatenate([qseg] * (K_ROWS // 128), axis=1)
        low, high = span_ref[0, qi], span_ref[1, qi]

        for part, (kk, vv) in enumerate(((kb_ref, vb_ref), (k_ref, v_ref), (ka_ref, va_ref))):
            def k_step(ki, _, part=part, kk=kk, vv=vv):
                k_at = pl.ds(pl.multiple_of(ki * K_ROWS, K_ROWS), K_ROWS)
                same = qseg == kseg_ref[part * per_part + ki]
                for h in range(heads):
                    cols = pl.ds(h * HEAD_DIM, HEAD_DIM)
                    s = lax.dot_general(q_ref[q_at, cols], kk[k_at, cols], (((1,), (1,)), ((), ())),
                                        preferred_element_type=jnp.float32) * factor
                    s = jnp.where(same, s, -1e30)
                    old = max_ref[h]
                    new = jnp.maximum(old, jnp.max(s, axis=1, keepdims=True))
                    max_ref[h] = new
                    wide = jnp.concatenate([new] * (K_ROWS // 128), axis=1)
                    p = jnp.exp2(s - wide).astype(jnp.bfloat16)
                    fade = jnp.exp2(old - new)
                    v_ext = jnp.concatenate([vv[k_at, cols], ones], axis=1)
                    acc_ref[h] = acc_ref[h] * jnp.concatenate([fade, fade], axis=1) + jnp.dot(
                        p, v_ext, preferred_element_type=jnp.float32)
                return 0

            first = jnp.clip(low - part * per_part, 0, per_part)
            last = jnp.clip(high - part * per_part, 0, per_part)
            lax.fori_loop(first, last, k_step, 0)
        for h in range(heads):
            acc = acc_ref[h]
            out_ref[q_at, h * HEAD_DIM:(h + 1) * HEAD_DIM] = (
                acc[:, :HEAD_DIM] / acc[:, HEAD_DIM:]).astype(jnp.bfloat16)
        return 0

    lax.fori_loop(0, rows // Q_ROWS, q_step, 0)


def attend(span, queries, keys, values, before, after, q_seg, k_seg, chunk, width):
    rows = queries.shape[0]
    heads = next(n for n in (4, 3, 2, 1) if (width // HEAD_DIM) % n == 0)
    block = heads * HEAD_DIM
    steps = width // block
    whole = pl.BlockSpec((rows, block), lambda i, s: (0, chunk * steps + i))
    k_part = pl.BlockSpec((rows, block), lambda i, s: (0, i))
    v_part = pl.BlockSpec((rows, block), lambda i, s: (0, steps + i))
    return pl.pallas_call(
        functools.partial(attend_kernel, heads=heads, rows=rows),
        grid_spec=pltpu.PrefetchScalarGridSpec(
            num_scalar_prefetch=1,
            grid=(steps,),
            in_specs=[whole, k_part, whole, k_part, v_part, whole, v_part,
                      pl.BlockSpec((rows, 128), lambda i, s: (0, 0)),
                      pl.BlockSpec((3 * rows // K_ROWS, 1, K_ROWS), lambda i, s: (0, 0, 0))],
            out_specs=pl.BlockSpec((rows, block), lambda i, s: (0, i)),
            scratch_shapes=[pltpu.VMEM((heads, Q_ROWS, 2 * HEAD_DIM), jnp.float32),
                            pltpu.VMEM((heads, Q_ROWS, HEAD_DIM), jnp.float32)],
        ),
        out_shape=jax.ShapeDtypeStruct((rows, width), jnp.bfloat16),
        compiler_params=pltpu.CompilerParams(vmem_limit_bytes=40 * 2 ** 20),
        cost_estimate=pl.CostEstimate(flops=32 * rows * rows * width, bytes_accessed=16 * rows * width,
                                      transcendentals=rows * rows * width // HEAD_DIM),
    )(span, queries, before, keys, after, before, values, after, q_seg, k_seg)


def shards(queries, keys, values, patch_counts, out_weight):
    rows, columns = queries.shape
    devices, groups = lax.axis_size("dp"), lax.axis_size("mp")
    width = columns // CHUNKS
    up = [(i, i + 1) for i in range(devices - 1)]
    down = [(j, i) for i, j in up]

    halos = []
    for c in range(CHUNKS):
        at = slice(c * width, (c + 1) * width)
        pair = jnp.concatenate([keys[:, at], values[:, at]], axis=1)
        halos.append((lax.ppermute(pair, "dp", up), lax.ppermute(pair, "dp", down)))

    row_first = lax.axis_index("dp") * rows
    total_rows = devices * rows
    ends = jnp.cumsum(patch_counts)
    starts = ends - patch_counts
    k_pos = row_first - rows + jnp.arange(3 * rows, dtype=jnp.int32)
    seg = jnp.sum((starts[None, :] <= k_pos[:, None]).astype(jnp.int32), axis=1) - 1
    seg = jnp.where((k_pos >= 0) & (k_pos < total_rows), seg, -1)
    q_seg = jnp.broadcast_to(seg[rows:2 * rows, None], (rows, 128))
    k_seg = seg.reshape(3 * rows // K_ROWS, 1, K_ROWS)
    q_first = row_first + jnp.arange(rows // Q_ROWS, dtype=jnp.int32) * Q_ROWS
    low = jnp.max(jnp.where(starts[None, :] <= q_first[:, None], starts[None, :], 0), axis=1)
    q_last = q_first + Q_ROWS - 1
    high = jnp.min(jnp.where(ends[None, :] > q_last[:, None], ends[None, :], total_rows), axis=1)
    low = jnp.clip((low - row_first + rows) // K_ROWS, 0, 3 * rows // K_ROWS)
    high = jnp.clip((high - row_first + rows + K_ROWS - 1) // K_ROWS, 0, 3 * rows // K_ROWS)
    span = jnp.stack([low, high]).astype(jnp.int32)

    chips = devices // 2
    ring = list(range(0, chips, 2)) + list(range(chips - 1 - chips % 2, 0, -2))
    onward = [(ring[i], ring[(i + 1) % chips]) for i in range(chips)]
    turn = [(2 * a, 2 * b) for a, b in onward] + [(2 * b + 1, 2 * a + 1) for a, b in onward]
    swap = [(i, i ^ 1) for i in range(devices)]
    part = out_weight.shape[1]
    block = rows // groups
    me = lax.axis_index("mp")

    weights = [out_weight]
    for step in range(1, chips):
        weights.append(lax.ppermute(weights[-1], "dp", turn))
    both = jnp.zeros((2, rows, columns), jnp.bfloat16)
    for c in range(CHUNKS):
        own = attend(span, queries, keys, values, *halos[c], q_seg, k_seg, c, width)
        other = lax.ppermute(own, "dp", swap)
        both = lax.dynamic_update_slice(both, own[None], (0, 0, c * width))
        both = lax.dynamic_update_slice(both, other[None], (1, 0, c * width))
    both = both.reshape(2 * rows, columns)

    mine, theirs, batch = [], [], []
    for step in range(chips):
        partial_value = jnp.dot(both, weights[step], preferred_element_type=jnp.float32)
        partial_value = partial_value.astype(jnp.bfloat16).reshape(2, groups, block, part)
        total = lax.dynamic_index_in_dim(partial_value, me, 1, False).astype(jnp.float32)
        for k in range(1, groups):
            away = lax.dynamic_index_in_dim(partial_value, (me + k) % groups, 1, False)
            got = lax.ppermute(away, "mp", [(i, (i + k) % groups) for i in range(groups)])
            total = total + got.astype(jnp.float32)
        total = total.astype(jnp.bfloat16)
        mine.append(total[0])
        batch.append(total[1])
        if step % (chips // 2) == chips // 2 - 1:
            theirs.append(lax.ppermute(jnp.stack(batch), "dp", swap))
            batch = []
    mine = jnp.stack(mine)

    place = jnp.array([ring.index(c) for c in range(chips)], jnp.int32)
    index = lax.axis_index("dp")
    core, at = index % 2, place[index // 2]
    owner = jnp.arange(devices, dtype=jnp.int32)
    ahead = (at - place[owner // 2]) % chips
    behind = (place[owner // 2] - at) % chips
    step_of = jnp.where(owner % 2 == 0, ahead, behind)
    return assemble(mine, *theirs, step_of, core)


def assemble_kernel(mine_at, early_at, late_at, is_late, core_ref, mine_ref, early_ref, late_ref, out_ref):
    part = mine_ref.shape[2]
    late = is_late[pl.program_id(0)]
    theirs = jnp.where(late == 1, late_ref[0], early_ref[0])

    @pl.when(core_ref[0] == 0)
    def _():
        out_ref[:, :part] = mine_ref[0]
        out_ref[:, part:] = theirs

    @pl.when(core_ref[0] == 1)
    def _():
        out_ref[:, :part] = theirs
        out_ref[:, part:] = mine_ref[0]


def assemble(mine, early, late, step_of, core):
    chips, block, part = mine.shape
    devices = 2 * chips
    if part % 128:
        owner = jnp.arange(devices, dtype=jnp.int32)
        pieces = jnp.concatenate([mine, early, late], axis=0)
        pieces = pieces[step_of + jnp.where(owner % 2 == core, 0, chips)]
        return jnp.transpose(pieces, (1, 0, 2)).reshape(block, devices * part)
    half = early.shape[0]
    pairs = step_of.reshape(chips, 2)
    mine_at = jnp.where(core == 0, pairs[:, 0], pairs[:, 1])
    theirs_at = jnp.where(core == 0, pairs[:, 1], pairs[:, 0])
    early_at, late_at = jnp.minimum(theirs_at, half - 1), jnp.maximum(theirs_at - half, 0)
    is_late = (theirs_at >= half).astype(jnp.int32)
    return pl.pallas_call(
        assemble_kernel,
        grid_spec=pltpu.PrefetchScalarGridSpec(
            num_scalar_prefetch=5,
            grid=(chips,),
            in_specs=[pl.BlockSpec((1, block, part), lambda d, m, e, l, i, c: (m[d], 0, 0)),
                      pl.BlockSpec((1, block, part), lambda d, m, e, l, i, c: (e[d], 0, 0)),
                      pl.BlockSpec((1, block, part), lambda d, m, e, l, i, c: (l[d], 0, 0))],
            out_specs=pl.BlockSpec((block, 2 * part), lambda d, m, e, l, i, c: (0, d)),
        ),
        out_shape=jax.ShapeDtypeStruct((block, devices * part), jnp.bfloat16),
        cost_estimate=pl.CostEstimate(flops=0, bytes_accessed=4 * block * devices * part, transcendentals=0),
    )(mine_at, early_at, late_at, is_late, core[None].astype(jnp.int32), mine, early, late)


def solution(mesh):
    placed = (P("dp", "mp"), P("dp", "mp"), P("dp", "mp"), P(), P("mp", "dp"))
    return jax.shard_map(
        shards, mesh=mesh, in_specs=placed, out_specs=P(("dp", "mp"), None), check_vma=False
    )
```

```python
import functools

import jax
import jax.numpy as jnp
from jax import lax
from jax.experimental import pallas as pl
from jax.experimental.pallas import tpu as pltpu
from jax.sharding import PartitionSpec as P

HEAD_DIM = 128
Q_ROWS = 256
K_ROWS = 256
CHUNKS = 2
LOG2E = 1.4426950408889634


def attend_kernel(span_ref, q_ref, kb_ref, k_ref, ka_ref, vb_ref, v_ref, va_ref, qseg_ref, kseg_ref, out_ref,
                  acc_ref, max_ref, *, heads, rows):
    factor = HEAD_DIM ** (-0.5) * LOG2E
    per_part = rows // K_ROWS
    ones = jnp.ones((K_ROWS, HEAD_DIM), jnp.bfloat16)

    def q_step(qi, _):
        q_at = pl.ds(pl.multiple_of(qi * Q_ROWS, Q_ROWS), Q_ROWS)
        acc_ref[...] = jnp.zeros_like(acc_ref)
        max_ref[...] = jnp.full_like(max_ref, -1e30)
        qseg = qseg_ref[q_at, :]
        qseg = jnp.concatenate([qseg] * (K_ROWS // 128), axis=1)
        low, high = span_ref[0, qi], span_ref[1, qi]

        for part, (kk, vv) in enumerate(((kb_ref, vb_ref), (k_ref, v_ref), (ka_ref, va_ref))):
            def k_step(ki, _, part=part, kk=kk, vv=vv):
                k_at = pl.ds(pl.multiple_of(ki * K_ROWS, K_ROWS), K_ROWS)
                same = qseg == kseg_ref[part * per_part + ki]
                for h in range(heads):
                    cols = pl.ds(h * HEAD_DIM, HEAD_DIM)
                    s = lax.dot_general(q_ref[q_at, cols], kk[k_at, cols], (((1,), (1,)), ((), ())),
                                        preferred_element_type=jnp.float32) * factor
                    s = jnp.where(same, s, -1e30)
                    old = max_ref[h]
                    new = jnp.maximum(old, jnp.max(s, axis=1, keepdims=True))
                    max_ref[h] = new
                    wide = jnp.concatenate([new] * (K_ROWS // 128), axis=1)
                    p = jnp.exp2(s - wide).astype(jnp.bfloat16)
                    fade = jnp.exp2(old - new)
                    v_ext = jnp.concatenate([vv[k_at, cols], ones], axis=1)
                    acc_ref[h] = acc_ref[h] * jnp.concatenate([fade, fade], axis=1) + jnp.dot(
                        p, v_ext, preferred_element_type=jnp.float32)
                return 0

            first = jnp.clip(low - part * per_part, 0, per_part)
            last = jnp.clip(high - part * per_part, 0, per_part)
            lax.fori_loop(first, last, k_step, 0)
        for h in range(heads):
            acc = acc_ref[h]
            out_ref[q_at, h * HEAD_DIM:(h + 1) * HEAD_DIM] = (
                acc[:, :HEAD_DIM] / acc[:, HEAD_DIM:]).astype(jnp.bfloat16)
        return 0

    lax.fori_loop(0, rows // Q_ROWS, q_step, 0)


def attend(span, queries, keys, values, before, after, q_seg, k_seg, chunk, width):
    rows = queries.shape[0]
    heads = next(n for n in (4, 3, 2, 1) if (width // HEAD_DIM) % n == 0)
    block = heads * HEAD_DIM
    steps = width // block
    whole = pl.BlockSpec((rows, block), lambda i, s: (0, chunk * steps + i))
    k_part = pl.BlockSpec((rows, block), lambda i, s: (0, i))
    v_part = pl.BlockSpec((rows, block), lambda i, s: (0, steps + i))
    return pl.pallas_call(
        functools.partial(attend_kernel, heads=heads, rows=rows),
        grid_spec=pltpu.PrefetchScalarGridSpec(
            num_scalar_prefetch=1,
            grid=(steps,),
            in_specs=[whole, k_part, whole, k_part, v_part, whole, v_part,
                      pl.BlockSpec((rows, 128), lambda i, s: (0, 0)),
                      pl.BlockSpec((3 * rows // K_ROWS, 1, K_ROWS), lambda i, s: (0, 0, 0))],
            out_specs=pl.BlockSpec((rows, block), lambda i, s: (0, i)),
            scratch_shapes=[pltpu.VMEM((heads, Q_ROWS, 2 * HEAD_DIM), jnp.float32),
                            pltpu.VMEM((heads, Q_ROWS, HEAD_DIM), jnp.float32)],
        ),
        out_shape=jax.ShapeDtypeStruct((rows, width), jnp.bfloat16),
        compiler_params=pltpu.CompilerParams(vmem_limit_bytes=40 * 2 ** 20),
        cost_estimate=pl.CostEstimate(flops=32 * rows * rows * width, bytes_accessed=16 * rows * width,
                                      transcendentals=rows * rows * width // HEAD_DIM),
    )(span, queries, before, keys, after, before, values, after, q_seg, k_seg)


def shards(queries, keys, values, patch_counts, out_weight):
    rows, columns = queries.shape
    devices, groups = lax.axis_size("dp"), lax.axis_size("mp")
    width = columns // CHUNKS
    up = [(i, i + 1) for i in range(devices - 1)]
    down = [(j, i) for i, j in up]

    halos = []
    for c in range(CHUNKS):
        at = slice(c * width, (c + 1) * width)
        pair = jnp.concatenate([keys[:, at], values[:, at]], axis=1)
        halos.append((lax.ppermute(pair, "dp", up), lax.ppermute(pair, "dp", down)))

    row_first = lax.axis_index("dp") * rows
    total_rows = devices * rows
    ends = jnp.cumsum(patch_counts)
    starts = ends - patch_counts
    k_pos = row_first - rows + jnp.arange(3 * rows, dtype=jnp.int32)
    seg = jnp.sum((starts[None, :] <= k_pos[:, None]).astype(jnp.int32), axis=1) - 1
    seg = jnp.where((k_pos >= 0) & (k_pos < total_rows), seg, -1)
    q_seg = jnp.broadcast_to(seg[rows:2 * rows, None], (rows, 128))
    k_seg = seg.reshape(3 * rows // K_ROWS, 1, K_ROWS)
    q_first = row_first + jnp.arange(rows // Q_ROWS, dtype=jnp.int32) * Q_ROWS
    low = jnp.max(jnp.where(starts[None, :] <= q_first[:, None], starts[None, :], 0), axis=1)
    q_last = q_first + Q_ROWS - 1
    high = jnp.min(jnp.where(ends[None, :] > q_last[:, None], ends[None, :], total_rows), axis=1)
    low = jnp.clip((low - row_first + rows) // K_ROWS, 0, 3 * rows // K_ROWS)
    high = jnp.clip((high - row_first + rows + K_ROWS - 1) // K_ROWS, 0, 3 * rows // K_ROWS)
    span = jnp.stack([low, high]).astype(jnp.int32)

    chips = devices // 2
    ring = list(range(0, chips, 2)) + list(range(chips - 1 - chips % 2, 0, -2))
    onward = [(ring[i], ring[(i + 1) % chips]) for i in range(chips)]
    turn = [(2 * a, 2 * b) for a, b in onward] + [(2 * b + 1, 2 * a + 1) for a, b in onward]
    swap = [(i, i ^ 1) for i in range(devices)]
    part = out_weight.shape[1]
    block = rows // groups
    me = lax.axis_index("mp")

    weights = [out_weight]
    for step in range(1, chips):
        weights.append(lax.ppermute(weights[-1], "dp", turn))
    both = jnp.zeros((2, rows, columns), jnp.bfloat16)
    for c in range(CHUNKS):
        if c:
            zero = (weights[min(2 * c, chips - 1)][0, 0].astype(jnp.float32) * 0.0).astype(jnp.int32)
            span = span + zero
        own = attend(span, queries, keys, values, *halos[c], q_seg, k_seg, c, width)
        other = lax.ppermute(own, "dp", swap)
        both = lax.dynamic_update_slice(both, own[None], (0, 0, c * width))
        both = lax.dynamic_update_slice(both, other[None], (1, 0, c * width))
    both = both.reshape(2 * rows, columns)

    mine, theirs, batch = [], [], []
    for step in range(chips):
        partial_value = jnp.dot(both, weights[step], preferred_element_type=jnp.float32)
        partial_value = partial_value.astype(jnp.bfloat16).reshape(2, groups, block, part)
        total = lax.dynamic_index_in_dim(partial_value, me, 1, False).astype(jnp.float32)
        for k in range(1, groups):
            away = lax.dynamic_index_in_dim(partial_value, (me + k) % groups, 1, False)
            got = lax.ppermute(away, "mp", [(i, (i + k) % groups) for i in range(groups)])
            total = total + got.astype(jnp.float32)
        total = total.astype(jnp.bfloat16)
        mine.append(total[0])
        batch.append(total[1])
        if step % (chips // 2) == chips // 2 - 1:
            theirs.append(lax.ppermute(jnp.stack(batch), "dp", swap))
            batch = []
    mine = jnp.stack(mine)

    place = jnp.array([ring.index(c) for c in range(chips)], jnp.int32)
    index = lax.axis_index("dp")
    core, at = index % 2, place[index // 2]
    owner = jnp.arange(devices, dtype=jnp.int32)
    ahead = (at - place[owner // 2]) % chips
    behind = (place[owner // 2] - at) % chips
    step_of = jnp.where(owner % 2 == 0, ahead, behind)
    return assemble(mine, *theirs, step_of, core)


def assemble_kernel(mine_at, early_at, late_at, is_late, core_ref, mine_ref, early_ref, late_ref, out_ref):
    part = mine_ref.shape[2]
    late = is_late[pl.program_id(0)]
    theirs = jnp.where(late == 1, late_ref[0], early_ref[0])

    @pl.when(core_ref[0] == 0)
    def _():
        out_ref[:, :part] = mine_ref[0]
        out_ref[:, part:] = theirs

    @pl.when(core_ref[0] == 1)
    def _():
        out_ref[:, :part] = theirs
        out_ref[:, part:] = mine_ref[0]


def assemble(mine, early, late, step_of, core):
    chips, block, part = mine.shape
    devices = 2 * chips
    if part % 128:
        owner = jnp.arange(devices, dtype=jnp.int32)
        pieces = jnp.concatenate([mine, early, late], axis=0)
        pieces = pieces[step_of + jnp.where(owner % 2 == core, 0, chips)]
        return jnp.transpose(pieces, (1, 0, 2)).reshape(block, devices * part)
    half = early.shape[0]
    pairs = step_of.reshape(chips, 2)
    mine_at = jnp.where(core == 0, pairs[:, 0], pairs[:, 1])
    theirs_at = jnp.where(core == 0, pairs[:, 1], pairs[:, 0])
    early_at, late_at = jnp.minimum(theirs_at, half - 1), jnp.maximum(theirs_at - half, 0)
    is_late = (theirs_at >= half).astype(jnp.int32)
    return pl.pallas_call(
        assemble_kernel,
        grid_spec=pltpu.PrefetchScalarGridSpec(
            num_scalar_prefetch=5,
            grid=(chips,),
            in_specs=[pl.BlockSpec((1, block, part), lambda d, m, e, l, i, c: (m[d], 0, 0)),
                      pl.BlockSpec((1, block, part), lambda d, m, e, l, i, c: (e[d], 0, 0)),
                      pl.BlockSpec((1, block, part), lambda d, m, e, l, i, c: (l[d], 0, 0))],
            out_specs=pl.BlockSpec((block, 2 * part), lambda d, m, e, l, i, c: (0, d)),
        ),
        out_shape=jax.ShapeDtypeStruct((block, devices * part), jnp.bfloat16),
        cost_estimate=pl.CostEstimate(flops=0, bytes_accessed=4 * block * devices * part, transcendentals=0),
    )(mine_at, early_at, late_at, is_late, core[None].astype(jnp.int32), mine, early, late)


def solution(mesh):
    placed = (P("dp", "mp"), P("dp", "mp"), P("dp", "mp"), P(), P("mp", "dp"))
    return jax.shard_map(
        shards, mesh=mesh, in_specs=placed, out_specs=P(("dp", "mp"), None), check_vma=False
    )
```
